128 devices in a mesh: rep: 16 (over y, x), shard: 8 (over z, core).
Axes of the slice: x: 4, y: 4, z: 4, core: 2. Of those that a mesh axis runs over, the one named last changes fastest.
Arguments:
- grads: bfloat16 [16, 8, 1408, 2048], P('rep', None, 'shard'), may hold values from -6 to 6
- momentum: float32 [8, 1408, 2048], P(None, 'shard', 'rep'), may hold values from -700 to 700
- owner: int32 [8], replicated, may hold values from 0 to 7, as said below
Outputs:
- new_momentum: float32 [8, 1408, 2048], P(None, 'shard', 'rep')
- update: bfloat16 [8, 1408, 2048], P(None, 'shard', 'rep')
- owned_blocks: bfloat16 [8, 2, 1408, 2048], P('shard', None, 'rep')
The draws below stay inside these ranges and needn't reach their ends.
Inputs may be any that keep to these rules, and one draw needn't show every extreme that they name: No owner index is named by more than 2 matrices; in every draw some owner index is named by exactly 2.
All inputs are finite; a program needn't handle non-finite values.
Results may differ from the reference program's by a relative error of at most 0.035.
Values may be sent and summed in bfloat16 or wider, within the bound.
No kernel may reach another device: no remote copies, remote signals or barrier semaphores. Data moves between devices by JAX's collectives and lax.ppermute only.
A program may use at most 64 MiB of HBM per device.

```python
import math
import jax
import jax.numpy as jnp
from jax import lax

D = 2048
FF = 1408
CAP = 2
ITERS = 2
REPS = 16
OWNERS = 8
MATS = 8


def draw_owner(key, part):
    key = jax.random.fold_in(key, 7)
    key_owner, key_scores, key_order = jax.random.split(key, 3)
    slot_count = MATS * CAP
    full_owner = jax.random.randint(key_owner, (), 0, MATS)
    scores = jax.random.permutation(key_scores, slot_count).astype(jnp.int32)
    slot_list = jnp.arange(slot_count, dtype=jnp.int32)
    scores = jnp.where(slot_list == 0, -CAP - 2, scores)
    scores = jnp.where(slot_list == (MATS - 1) * CAP, -CAP - 1, scores)
    scores = jnp.where(slot_list // CAP == full_owner, slot_list % CAP - CAP, scores)
    ordering = jnp.argsort(scores, stable=True).astype(jnp.int32)
    picked = ordering[:MATS] // CAP
    shuffle = jax.random.permutation(key_order, MATS)
    return picked[shuffle].astype(jnp.int32)


def rising_scales(key, count, top):
    position = jnp.arange(count, dtype=jnp.float32) / max(count - 1, 1)
    rough = jax.random.uniform(key, (count,), jnp.float32, 0.8, 1.25)
    return jnp.power(top, position) * rough


def draw_momentum(key, part):
    key = jax.random.fold_in(key, 11)
    key_base, key_rows, key_cols = jax.random.split(key, 3)
    top = 10.0
    base = jax.random.truncated_normal(key_base, -4.0, 4.0, (MATS, FF, D), jnp.float32)
    row_scale = rising_scales(key_rows, FF, top)
    col_scale = rising_scales(key_cols, D, top)
    return base * row_scale[None, :, None] * col_scale[None, None, :]


def with_spikes(result, rng, source, target, parts, factor):
    def block_of(axis_at):
        return (jnp.arange(result.shape[axis_at]) // (result.shape[axis_at] // parts)).reshape((-1,) + (1,) * (result.ndim - 1 - axis_at))

    one_side = jax.random.permutation(rng, parts)[block_of(target)]
    far = (block_of(target) + parts // 2) % parts
    return jnp.where((block_of(source) == one_side) | (block_of(source) == far), factor * result, result)


def levels(own_key, shape, cuts, least, top_value):
    factor_of, own = 1.0, jax.random.fold_in(own_key, 6)
    for dim, blocks in cuts:
        draws = jnp.exp(jax.random.uniform(jax.random.fold_in(own, dim), (blocks,), jnp.float32, least / len(cuts), top_value / len(cuts)))
        factor_of = factor_of * jnp.repeat(draws, shape[dim] // blocks).reshape([-1 if axis == dim else 1 for axis in range(len(shape))])
    return factor_of


def bell_draw_with(own_key, shape, spread, limit, pieces, heavy, kind=jnp.bfloat16):
    entries = spread * jax.random.normal(own_key, shape, jnp.float32)
    if pieces:
        entries = entries * levels(own_key, shape, pieces, -0.22, 0.18)
    return jnp.clip(with_spikes(entries, jax.random.fold_in(own_key, 3), *heavy), -limit, limit).astype(kind)


def setup_inputs(seed: int = 0) -> dict:
    arg_keys = jax.random.split(jax.random.key(seed), 4)
    return {
        "grads": bell_draw_with(arg_keys[0], (REPS, MATS, FF, D), 1.0, 6.0, ((0, 16), (2, 8)), (0, 3, 16, 2.0)),
        "momentum": draw_momentum(jax.random.fold_in(arg_keys[3], 71), 0),
        "owner": draw_owner(jax.random.fold_in(arg_keys[3], 71), 0),
    }


decay_rate = 0.95
spectral_gain = 0.75
epsilon = 1e-06

def slot_matrix(owner, owner_count, capacity):
    matrix_index = jnp.arange(owner.shape[0], dtype=jnp.int32)
    same_owner = owner[:, None] == owner[None, :]
    before_me = matrix_index[None, :] < matrix_index[:, None]
    position = lax.optimization_barrier(jnp.sum((same_owner & before_me).astype(jnp.int32), axis=1))
    slot_index = owner * capacity + position
    slot_list = jnp.arange(owner_count * capacity, dtype=jnp.int32)
    return (slot_index[None, :] == slot_list[:, None]).astype(jnp.int32)

def orthogonalize(advance):
    rounded = advance.astype(jnp.bfloat16).astype(jnp.float32)
    squares = jnp.sum(rounded * rounded)
    factor = spectral_gain * math.sqrt(FF * D) / jnp.sqrt(squares + epsilon)
    current = (rounded * factor).astype(jnp.bfloat16)
    for iteration in range(ITERS):
        gram = (jnp.dot(current, current.T, preferred_element_type=jnp.float32) / D).astype(jnp.bfloat16)
        product = jnp.dot(gram, current, preferred_element_type=jnp.float32)
        current = (1.5 * current.astype(jnp.float32) - 0.5 * product).astype(jnp.bfloat16)
    return current

def reference(grads, momentum, owner):

    def per_matrix(pair):
        grad_stack, state = pair
        summed = lax.optimization_barrier(jnp.sum(grad_stack.astype(jnp.float32), axis=0))
        new_state = decay_rate * state + summed
        advance = summed + decay_rate * new_state
        return (new_state, orthogonalize(advance))
    new_momentum, update = lax.map(per_matrix, (jnp.moveaxis(grads, 1, 0), momentum))
    table = slot_matrix(owner, OWNERS, CAP)
    filled = lax.optimization_barrier(jnp.sum(table, axis=1))
    chosen = lax.optimization_barrier(jnp.sum(table * jnp.arange(MATS, dtype=jnp.int32)[None, :], axis=1)).astype(jnp.int32)
    picked = update[chosen]
    owned = jnp.where(filled[:, None, None] > 0, picked, jnp.zeros_like(picked))
    return (new_momentum, update, owned.reshape(OWNERS, CAP, FF, D))
```

```python
import math

import jax
import jax.numpy as jnp
from jax import lax
from jax.experimental import pallas as pl
from jax.experimental.pallas import tpu as pltpu
from jax.sharding import PartitionSpec as P

D = 2048
FF = 1408
CAP = 2
MATS = 8
SIDE = 4
ROWS = FF // 8
COLS = D // 16
STRIP = FF // 16
VMEM = 56 * 1024 * 1024

decay_rate = 0.95
spectral_gain = 0.75
epsilon = 1e-06

BF = jnp.bfloat16
F32 = jnp.float32


def along_z(step):
    return [(z * 2 + c, (z + step) % 4 * 2 + c) for z in range(4) for c in range(2)]


def along(phase, step):
    pairs = []
    for y in range(SIDE):
        for x in range(SIDE):
            for shard in range(8):
                to_x = (x + step) % SIDE if shard % 2 == phase else x
                to_y = y if shard % 2 == phase else (y + step) % SIDE
                pairs.append(((y * SIDE + x) * 8 + shard, (to_y * SIDE + to_x) * 8 + shard))
    return pairs


def place():
    rep = lax.axis_index("rep")
    y, x = rep // SIDE, rep % SIDE
    core = lax.axis_index("shard") % 2
    return jnp.where(core == 0, x, y), jnp.where(core == 0, y, x), core


def block_of(early, late, core):
    return jnp.where(core == 0, late * SIDE + early, early * SIDE + late)


def params():
    return pltpu.CompilerParams(vmem_limit_bytes=VMEM)


def block_columns(block):
    return pl.ds(pl.multiple_of(block * COLS, COLS), COLS)


def split_kernel(steps, grads, *outs):
    early, _, core = place()
    for step, out in zip(steps, outs):
        for late in range(SIDE):
            out[late, 0] = grads[0, :, block_columns(block_of((early + step) % SIDE, late, core))]


def split(grads, steps):
    return pl.pallas_call(
        lambda *refs: split_kernel(steps, *refs),
        out_shape=[jax.ShapeDtypeStruct((SIDE, MATS, ROWS, COLS), BF)] * len(steps),
        grid=(MATS,),
        in_specs=[pl.BlockSpec((1, ROWS, D), lambda m: (m, 0, 0))],
        out_specs=[pl.BlockSpec((SIDE, 1, ROWS, COLS), lambda m: (0, m, 0, 0))] * len(steps),
        compiler_params=params(),
        name="split",
    )(grads)


def first_sum_kernel(*refs):
    parts, outs = refs[:4], refs[4:]
    _, late, _ = place()
    for step in range(SIDE):
        at = (late + step) % SIDE
        total = parts[0][at, 0].astype(F32)
        for part in parts[1:]:
            total = total + part[at, 0].astype(F32)
        outs[step][0] = total.astype(BF)


def first_sum(parts):
    return pl.pallas_call(
        first_sum_kernel,
        out_shape=[jax.ShapeDtypeStruct((MATS, ROWS, COLS), BF)] * SIDE,
        grid=(MATS,),
        in_specs=[pl.BlockSpec((SIDE, 1, ROWS, COLS), lambda m: (0, m, 0, 0))] * 4,
        out_specs=[pl.BlockSpec((1, ROWS, COLS), lambda m: (m, 0, 0))] * SIDE,
        compiler_params=params(),
        name="first_sum",
    )(*parts)


def second_sum_kernel(*refs):
    parts, (momentum, new_momentum, rounded) = refs[:4], refs[4:]
    total = parts[0][...].astype(F32)
    for part in parts[1:]:
        total = total + part[...].astype(F32)
    state = decay_rate * momentum[...] + total
    new_momentum[...] = state
    rounded[...] = (total + decay_rate * state).astype(BF)


def second_sum(parts, momentum):
    block = pl.BlockSpec((2, ROWS, COLS), lambda m: (m, 0, 0))
    return pl.pallas_call(
        second_sum_kernel,
        out_shape=[jax.ShapeDtypeStruct(momentum.shape, F32), jax.ShapeDtypeStruct(momentum.shape, BF)],
        grid=(MATS // 2,),
        in_specs=[block] * 5,
        out_specs=[block, block],
        compiler_params=params(),
        name="second_sum",
    )(*parts, momentum)


def newton_kernel(*refs):
    parts = refs[:4]
    own, rows_out, cols_out, whole, gram, sems = refs[4:]
    early, late, core = place()
    rep = block_of(early, late, core)
    copies = []
    for j in range(SIDE):
        for k in range(SIDE):
            block = block_of((early - k + SIDE) % SIDE, (late - j + SIDE) % SIDE, core)
            copies.append(
                pltpu.make_async_copy(parts[j].at[k], whole.at[:, block_columns(block)], sems.at[j, k])
            )
    for copy in copies:
        copy.start()
    for copy in copies:
        copy.wait()
    squares = jnp.zeros((), F32)
    for low in range(0, FF, 256):
        size = min(256, FF - low)
        panel = lax.dot_general(
            whole[...], whole[low : low + size, :], (((1,), (1,)), ((), ())), preferred_element_type=F32
        )
        corner = panel[low : low + size]
        on_line = lax.broadcasted_iota(jnp.int32, (size, size), 0) == lax.broadcasted_iota(
            jnp.int32, (size, size), 1
        )
        squares = squares + jnp.sum(jnp.where(on_line, corner, 0.0))
        gram[:, low : low + size] = panel.astype(BF)
    factor = spectral_gain * math.sqrt(FF * D) / jnp.sqrt(jnp.full((1, 1), squares) + epsilon)
    scale = factor * factor / D

    def strip_of(ref):
        window = ref[pl.ds(pl.multiple_of(rep // 2 * (2 * STRIP) + rep % 2 * (STRIP - 8), 16), STRIP + 8), :]
        window = window.astype(F32)
        return jnp.where(rep % 2 == 0, window[:STRIP], window[8:])

    start = own[...].astype(F32).T
    first = scale * jnp.dot(start.astype(BF), gram[...], preferred_element_type=F32)
    strip = scale * strip_of(gram)
    power = jnp.concatenate([first, strip], axis=0)
    for _ in range(3):
        product = jnp.dot(power.astype(BF), gram[...], preferred_element_type=F32)
        power = 1.5 * power - (0.5 * scale) * product
    columns = factor * (2.25 * start - 0.75 * first - 0.5 * power[:COLS])
    cols_out[...] = columns.T.astype(BF)
    mixed = (0.75 * strip + 0.5 * power[COLS:]).astype(BF)
    product = jnp.dot(mixed, whole[...], preferred_element_type=F32)
    rows_out[...] = (factor * (2.25 * strip_of(whole) - product)).astype(BF)


def newton(parts, own):
    anywhere = pl.BlockSpec(memory_space=pl.ANY)
    inside = pl.BlockSpec(memory_space=pltpu.VMEM)
    return pl.pallas_call(
        newton_kernel,
        out_shape=[jax.ShapeDtypeStruct((STRIP, D), BF), jax.ShapeDtypeStruct((FF, COLS), BF)],
        in_specs=[anywhere] * 4 + [inside],
        out_specs=[inside, inside],
        scratch_shapes=[
            pltpu.VMEM((FF, D), BF),
            pltpu.VMEM((FF, FF), BF),
            pltpu.SemaphoreType.DMA((SIDE, SIDE)),
        ],
        compiler_params=params(),
        name="newton",
    )(*parts, own)


def slots_of(owner, who):
    mine = owner == who
    count = jnp.sum(mine.astype(jnp.int32))
    index = jnp.arange(MATS, dtype=jnp.int32)
    first = jnp.min(jnp.where(mine, index, MATS))
    last = jnp.max(jnp.where(mine, index, -1))
    return (jnp.where(count > 0, first, 0), count > 0), (jnp.where(count > 1, last, 0), count > 1)


def pick(pieces, at):
    result = pieces[0]
    for number in range(1, len(pieces)):
        result = jnp.where(at == number, pieces[number], result)
    return result


def per_device(grads, momentum, owner):
    grads = grads[0]
    axes = ("rep", "shard")
    steps = (2, 1, 3)
    arrived = [lax.ppermute(piece, axes, along(0, n)) for n, piece in zip(steps, split(grads, steps))]
    sums = first_sum([*split(grads, (0,)), *arrived])
    final = [sums[0]] + [lax.ppermute(sums[n], axes, along(1, n)) for n in steps]
    new_momentum, rounded = second_sum(final, momentum)
    own = lax.all_to_all(rounded, "shard", 0, 0, tiled=True).reshape(FF, COLS)
    four = jnp.stack([own] + [lax.ppermute(own, axes, along(0, n)) for n in (1, 2, 3)])
    whole = [four] + [lax.ppermute(four, axes, along(1, n)) for n in (1, 2, 3)]
    strip, columns = newton(whole, own)
    shard = lax.axis_index("shard")
    floor, core = shard // 2, shard % 2
    pieces = [strip] + [lax.ppermute(strip, "shard", along_z(n)) for n in (1, 2, 3)]
    update = lax.all_to_all(columns.reshape(MATS, ROWS, COLS), "shard", 0, 0, tiled=True)
    other = [pick(pieces, (floor - m // 2) % 4) for m, _ in slots_of(owner, floor * 2 + 1 - core)]
    handed = lax.ppermute(jnp.stack(other), "shard", [(s, s ^ 1) for s in range(8)])
    owned = []
    for slot, (m, filled) in enumerate(slots_of(owner, shard)):
        found = jnp.where(m % 2 == core, pick(pieces, (floor - m // 2) % 4), handed[slot])
        owned.append(jnp.where(filled, found, jnp.zeros_like(found)))
    return new_momentum, update, jnp.stack(owned)[None]


def solution(mesh):
    placed = (P("rep", None, "shard", None), P(None, "shard", "rep"), P())
    return jax.shard_map(
        per_device,
        mesh=mesh,
        in_specs=placed,
        out_specs=(P(None, "shard", "rep"), P(None, "shard", "rep"), P("shard", None, "rep", None)),
        check_vma=False,
    )
```

```python
import math

import jax
import jax.numpy as jnp
from jax import lax
from jax.experimental import pallas as pl
from jax.experimental.pallas import tpu as pltpu
from jax.sharding import PartitionSpec as P

D = 2048
FF = 1408
CAP = 2
MATS = 8
SIDE = 4
ROWS = FF // 8
COLS = D // 16
STRIP = FF // 16
PANEL = 256

decay_rate = 0.95
spectral_gain = 0.75
epsilon = 1e-06

BF = jnp.bfloat16
F32 = jnp.float32


def along_z(step):
    return [(z * 2 + c, (z + step) % 4 * 2 + c) for z in range(4) for c in range(2)]


def along(phase, step):
    pairs = []
    for y in range(SIDE):
        for x in range(SIDE):
            for shard in range(8):
                to_x = (x + step) % SIDE if shard % 2 == phase else x
                to_y = y if shard % 2 == phase else (y + step) % SIDE
                pairs.append(((y * SIDE + x) * 8 + shard, (to_y * SIDE + to_x) * 8 + shard))
    return pairs


def place():
    rep = lax.axis_index("rep")
    y, x = rep // SIDE, rep % SIDE
    core = lax.axis_index("shard") % 2
    return jnp.where(core == 0, x, y), jnp.where(core == 0, y, x), core


def block_of(early, late, core):
    return jnp.where(core == 0, late * SIDE + early, early * SIDE + late)


def params(mebibytes):
    return pltpu.CompilerParams(vmem_limit_bytes=mebibytes * 1024 * 1024)


def block_columns(block):
    return pl.ds(pl.multiple_of(block * COLS, COLS), COLS)


def split_kernel(wanted, grads, *refs):
    outs, sems = refs[:-1], refs[-1]
    early, late, core = place()
    copies = []
    for out, steps in zip(outs, wanted):
        for number, (early_step, late_step) in enumerate(steps):
            block = block_of((early + early_step) % SIDE, (late + late_step) % SIDE, core)
            copies.append(
                pltpu.make_async_copy(grads.at[:, :, block_columns(block)], out.at[number], sems.at[len(copies)])
            )
    for copy in copies:
        copy.start()
    for copy in copies:
        copy.wait()


def split(grads, wanted):
    return pl.pallas_call(
        lambda *refs: split_kernel(wanted, *refs),
        out_shape=[jax.ShapeDtypeStruct((len(steps), MATS, ROWS, COLS), BF) for steps in wanted],
        in_specs=[pl.BlockSpec(memory_space=pl.ANY)],
        out_specs=[pl.BlockSpec(memory_space=pltpu.VMEM)] * len(wanted),
        scratch_shapes=[pltpu.SemaphoreType.DMA((sum(len(steps) for steps in wanted),))],
        compiler_params=params(6),
        name="split",
    )(grads)


def add(*parts):
    total = parts[0].astype(F32)
    for part in parts[1:]:
        total = total + part.astype(F32)
    return total


def panel_spans():
    return [(low, min(PANEL, FF - low)) for low in range(0, FF, PANEL)]


def panel_product(columns, low, size):
    return lax.dot_general(
        columns[low:, :], columns[low : low + size, :], (((1,), (1,)), ((), ())), preferred_element_type=F32
    )


def bring(pieces, columns, sems):
    copies = []
    for number, piece in enumerate(pieces):
        copies.append(
            pltpu.make_async_copy(piece, columns.at[:, pl.ds(number * COLS, COLS)], sems.at[number])
        )
    for copy in copies:
        copy.start()
    return copies


def flat(refs, shapes):
    views = []
    for ref, shape in zip(refs, shapes):
        views += [ref] if len(shape) == 2 else [ref.at[number] for number in range(shape[0])]
    return views


def gram_kernel(shapes, before, *refs):
    spans = panel_spans()
    pieces, refs = flat(refs[: len(shapes)], shapes), refs[len(shapes) :]
    old, refs = (refs[: len(spans)], refs[len(spans) :]) if before else (None, refs)
    new, (columns, sems) = refs[: len(spans)], refs[len(spans) :]
    for copy in bring(pieces, columns, sems):
        copy.wait()
    for number, (low, size) in enumerate(spans):
        product = panel_product(columns, low, size)
        new[number][...] = product + old[number][...] if before else product


def gram_part(pieces, before=()):
    shapes = [piece.shape for piece in pieces]
    count = sum(1 if len(shape) == 2 else shape[0] for shape in shapes)
    inside = pl.BlockSpec(memory_space=pltpu.VMEM)
    return pl.pallas_call(
        lambda *refs: gram_kernel(shapes, bool(before), *refs),
        out_shape=[jax.ShapeDtypeStruct((FF - low, size), F32) for low, size in panel_spans()],
        in_specs=[pl.BlockSpec(memory_space=pl.ANY)] * len(pieces) + [inside] * len(before),
        out_specs=[inside] * len(panel_spans()),
        scratch_shapes=[pltpu.VMEM((FF, count * COLS), BF), pltpu.SemaphoreType.DMA((count,))],
        compiler_params=params(24),
        name="gram",
    )(*pieces, *before)


def newton_kernel(shapes, places, fresh_at, *refs):
    spans = panel_spans()
    pieces, refs = flat(refs[: len(shapes)], shapes), refs[len(shapes) :]
    before, refs = refs[: len(spans)], refs[len(spans) :]
    own, rows_out, cols_out, whole, fresh, gram, sems, fresh_sems = refs
    early, late, core = place()
    floor = lax.axis_index("shard") // 2
    rep = block_of(early, late, core)
    fresh_copies = bring([pieces[number] for number in fresh_at], fresh, fresh_sems)
    copies = []
    for number, (k, j) in enumerate(places):
        block = block_of((early - k + SIDE) % SIDE, (late - j + SIDE) % SIDE, core)
        copies.append(pltpu.make_async_copy(pieces[number], whole.at[:, block_columns(block)], sems.at[number]))
    for copy in copies:
        copy.start()
    start = own[...].astype(F32).T
    for copy in fresh_copies:
        copy.wait()
    squares = jnp.zeros((), F32)
    for number, (low, size) in enumerate(spans):
        panel = panel_product(fresh, low, size)
        panel = panel + before[number][...]
        on_line = lax.broadcasted_iota(jnp.int32, (size, size), 0) == lax.broadcasted_iota(
            jnp.int32, (size, size), 1
        )
        squares = squares + jnp.sum(jnp.where(on_line, panel[:size], 0.0))
        panel = panel.astype(BF)
        gram[low:, low : low + size] = panel
        if low + size < FF:
            gram[low : low + size, low + size :] = panel[size:].T
    factor = spectral_gain * math.sqrt(FF * D) / jnp.sqrt(jnp.full((1, 1), squares) + epsilon)
    scale = factor * factor / D
    half = rep % 2
    layer = (floor - rep // 4 + SIDE) % SIDE
    flipped = (rep // 2 % 2 + core) % 2
    base = layer * (2 * ROWS) + flipped * ROWS + half * (STRIP - 8)

    def strip_of(ref):
        window = ref[pl.ds(pl.multiple_of(base, 16), STRIP + 8), :].astype(F32)
        return jnp.where(half == 0, window[:STRIP], window[8:])

    first = scale * jnp.dot(start.astype(BF), gram[...], preferred_element_type=F32)
    strip = scale * strip_of(gram)
    power = jnp.concatenate([first, strip], axis=0)
    for _ in range(3):
        product = jnp.dot(power.astype(BF), gram[...], preferred_element_type=F32)
        power = 1.5 * power - (0.5 * scale) * product
    mixed = (0.75 * strip + 0.5 * power[COLS:]).astype(BF)
    for copy in copies:
        copy.wait()
    product = jnp.dot(mixed, whole[...], preferred_element_type=F32)
    rows_out[...] = (factor * (2.25 * strip_of(whole) - product)).astype(BF)
    columns = (factor * (2.25 * start - 0.75 * first - 0.5 * power[:COLS])).T.astype(BF)
    for k in range(SIDE):
        for i in range(2):
            at = ((floor - k + SIDE) % SIDE * 2 + (core + i) % 2) * ROWS
            low = (2 * k + i) * ROWS
            cols_out[pl.ds(pl.multiple_of(at, 16), ROWS), :] = columns[low : low + ROWS]


def newton(pieces, places, fresh_at, before, own):
    shapes = [piece.shape for piece in pieces]
    anywhere = pl.BlockSpec(memory_space=pl.ANY)
    inside = pl.BlockSpec(memory_space=pltpu.VMEM)
    return pl.pallas_call(
        lambda *refs: newton_kernel(shapes, places, fresh_at, *refs),
        out_shape=[jax.ShapeDtypeStruct((STRIP, D), BF), jax.ShapeDtypeStruct((FF, COLS), BF)],
        in_specs=[anywhere] * len(pieces) + [inside] * (len(before) + 1),
        out_specs=[inside, inside],
        scratch_shapes=[
            pltpu.VMEM((FF, D), BF),
            pltpu.VMEM((FF, len(fresh_at) * COLS), BF),
            pltpu.VMEM((FF, FF), BF),
            pltpu.SemaphoreType.DMA((16,)),
            pltpu.SemaphoreType.DMA((len(fresh_at),)),
        ],
        compiler_params=params(26),
        name="newton",
    )(*pieces, *before, own)


def slots_of(owner, who):
    mine = owner == who
    count = jnp.sum(mine.astype(jnp.int32))
    index = jnp.arange(MATS, dtype=jnp.int32)
    first = jnp.min(jnp.where(mine, index, MATS))
    last = jnp.max(jnp.where(mine, index, -1))
    return (jnp.where(count > 0, first, 0), count > 0), (jnp.where(count > 1, last, 0), count > 1)


def choose_kernel(choice, *refs):
    pieces, out = refs[:-1], refs[-1]
    for slot in range(CAP):
        for number, piece in enumerate(pieces):

            @pl.when(choice[slot] == number)
            def _():
                out[0, slot] = piece[...] if len(piece.shape) == 2 else piece[0, slot]

        @pl.when(choice[slot] == len(pieces))
        def _():
            out[0, slot] = jnp.zeros((STRIP, D), BF)


def choose(choice, pieces):
    inside = pl.BlockSpec(memory_space=pltpu.VMEM)
    return pl.pallas_call(
        choose_kernel,
        out_shape=jax.ShapeDtypeStruct((1, CAP, STRIP, D), BF),
        in_specs=[pl.BlockSpec(memory_space=pltpu.SMEM)] + [inside] * len(pieces),
        out_specs=inside,
        compiler_params=params(8),
        name="choose",
    )(jnp.stack(choice).astype(jnp.int32), *pieces)


def per_device(grads, momentum, owner):
    grads = grads[0]
    axes = ("rep", "shard")

    def move(piece, phase, step):
        return lax.ppermute(piece, axes, along(phase, step))

    def cut(*wanted):
        return split(grads, [[(early, late) for late in lates] for early, lates in wanted])

    one, two = (3, 0), (2, 1)
    across_one, across_two = cut((2, one), (2, two))
    across_one, across_two = move(across_one, 0, 1), move(across_two, 0, 3)
    side_one, side_two = cut((3, one), (1, two))
    side_two, side_one = move(side_two, 0, 1), move(side_one, 0, 3)
    next_one, next_two = cut((1, one), (3, two))
    mine_one, mine_two = cut((0, one), (0, two))
    relay_one = move(add(next_one, across_one).astype(BF), 0, 1)
    relay_two = move(add(next_two, across_two).astype(BF), 0, 3)
    late_2 = move(add(mine_two[0], relay_two[0], side_two[0]).astype(BF), 1, 2)
    late_1 = move(add(mine_two[1], relay_two[1], side_two[1]).astype(BF), 1, 1)
    late_3 = move(add(mine_one[0], relay_one[0], side_one[0]).astype(BF), 1, 3)
    terms = (mine_one[1], relay_one[1], side_one[1], late_2, late_1, late_3)
    summed = add(*terms)
    rounded = (summed + decay_rate * (decay_rate * momentum + summed)).astype(BF)
    shard = lax.axis_index("shard")
    floor, core = shard // 2, shard % 2
    swap = [(s, s ^ 1) for s in range(8)]
    by_core = rounded.reshape(SIDE, 2, ROWS, COLS)
    mine = lax.dynamic_index_in_dim(by_core, core, 1, keepdims=False)
    theirs = lax.dynamic_index_in_dim(by_core, 1 - core, 1, keepdims=False)
    layers = jnp.stack([mine, lax.ppermute(theirs, "shard", swap)], axis=1)

    def layer(step):
        return lax.dynamic_index_in_dim(layers, (floor + step) % SIDE, 0, keepdims=False)

    parts = [layer(0)] + [lax.ppermute(layer(n), "shard", along_z(n)) for n in (1, 2, 3)]
    own = jnp.stack(parts).reshape(FF, COLS)
    line = jnp.stack([own, move(own, 0, 1), move(own, 0, 3), move(own, 0, 2)])
    ahead, behind = move(line, 1, 1), move(line, 1, 3)
    terms, _ = lax.optimization_barrier((terms, line))
    new_momentum = decay_rate * momentum + add(*terms)
    gram = gram_part([line])
    ahead, behind, gram, new_momentum = lax.optimization_barrier((ahead, behind, gram, new_momentum))
    across_a, across_b = move(ahead[:2], 1, 1), move(behind[2:], 1, 3)
    gram = gram_part([ahead, behind], gram)
    pieces = [line, ahead, behind, across_a, across_b]
    places = [(k, j) for j in (0, 1, 3, 2) for k in (0, 1, 3, 2)]
    strip, columns = newton(pieces, places, (12, 13, 14, 15), gram, own)
    pieces = [strip] + [lax.ppermute(strip, "shard", along_z(n)) for n in (1, 2, 3)]
    update = lax.all_to_all(columns.reshape(MATS, ROWS, COLS), "shard", 0, 0, tiled=True)
    pieces, update = lax.optimization_barrier((pieces, update))
    wanted = [(floor - m // 2 + 4) % 4 for m, _ in slots_of(owner, floor * 2 + 1 - core)]
    handed = lax.ppermute(choose(wanted, pieces), "shard", swap)
    choice = []
    for m, filled in slots_of(owner, shard):
        choice.append(jnp.where(filled, jnp.where(m % 2 == core, (floor - m // 2 + 4) % 4, 4), 5))
    return new_momentum, update, choose(choice, [*pieces, handed])


def solution(mesh):
    placed = (P("rep", None, "shard", None), P(None, "shard", "rep"), P())
    return jax.shard_map(
        per_device,
        mesh=mesh,
        in_specs=placed,
        out_specs=(P(None, "shard", "rep"), P(None, "shard", "rep"), P("shard", None, "rep", None)),
        check_vma=False,
    )
```

```python
import math

import jax
import jax.numpy as jnp
from jax import lax
from jax.experimental import pallas as pl
from jax.experimental.pallas import tpu as pltpu
from jax.sharding import PartitionSpec as P

D = 2048
FF = 1408
CAP = 2
MATS = 8
SIDE = 4
ROWS = FF // 8
COLS = D // 16
STRIP = FF // 16
HALF = FF // 2
PANEL = 256

decay_rate = 0.95
spectral_gain = 0.75
epsilon = 1e-06

BF = jnp.bfloat16
F32 = jnp.float32


def along_z(step):
    return [(z * 2 + c, (z + step) % 4 * 2 + c) for z in range(4) for c in range(2)]


def along(phase, step):
    pairs = []
    for y in range(SIDE):
        for x in range(SIDE):
            for shard in range(8):
                to_x = (x + step) % SIDE if shard % 2 == phase else x
                to_y = y if shard % 2 == phase else (y + step) % SIDE
                pairs.append(((y * SIDE + x) * 8 + shard, (to_y * SIDE + to_x) * 8 + shard))
    return pairs


def place():
    rep = lax.axis_index("rep")
    y, x = rep // SIDE, rep % SIDE
    core = lax.axis_index("shard") % 2
    return jnp.where(core == 0, x, y), jnp.where(core == 0, y, x), core


def block_of(early, late, core):
    return jnp.where(core == 0, late * SIDE + early, early * SIDE + late)


def params(mebibytes):
    return pltpu.CompilerParams(vmem_limit_bytes=mebibytes * 1024 * 1024)


def block_columns(block):
    return pl.ds(pl.multiple_of(block * COLS, COLS), COLS)


def split_kernel(wanted, grads, *refs):
    outs, sems = refs[:-1], refs[-1]
    early, late, core = place()
    copies = []
    for out, steps in zip(outs, wanted):
        for number, (early_step, late_step) in enumerate(steps):
            block = block_of((early + early_step) % SIDE, (late + late_step) % SIDE, core)
            for matrix in range(MATS):
                source, target = grads.at[matrix, :, block_columns(block)], out.at[number, matrix]
                copies.append(pltpu.make_async_copy(source, target, sems.at[len(copies)]))
    for copy in copies:
        copy.start()
    for copy in copies:
        copy.wait()


def split(grads, wanted):
    return pl.pallas_call(
        lambda *refs: split_kernel(wanted, *refs),
        out_shape=[jax.ShapeDtypeStruct((len(steps), MATS, ROWS, COLS), BF) for steps in wanted],
        in_specs=[pl.BlockSpec(memory_space=pltpu.HBM)],
        out_specs=[pl.BlockSpec(memory_space=pltpu.VMEM)] * len(wanted),
        scratch_shapes=[pltpu.SemaphoreType.DMA((MATS * sum(len(steps) for steps in wanted),))],
        compiler_params=params(4),
        name="split",
    )(grads)


def add(*parts):
    total = parts[0].astype(F32)
    for part in parts[1:]:
        total = total + part.astype(F32)
    return total


def panel_spans():
    return [(low, min(PANEL, FF - low)) for low in range(0, FF, PANEL)]


def panel_product(columns, low, size):
    return lax.dot_general(
        columns[low:, :], columns[low : low + size, :], (((1,), (1,)), ((), ())), preferred_element_type=F32
    )


def bring(pieces, columns, sems):
    copies = []
    for number, halves in enumerate(pieces):
        for half, piece in enumerate(halves):
            target = columns.at[pl.ds(half * HALF, HALF), pl.ds(number * COLS, COLS)]
            copies.append(pltpu.make_async_copy(piece, target, sems.at[number, half]))
    for copy in copies:
        copy.start()
    return copies


def flat(refs):
    views, upper = [], None
    for ref in refs:
        if ref.shape[1] == FF:
            views += [tuple(ref.at[n, pl.ds(half * HALF, HALF)] for half in range(2)) for n in range(ref.shape[0])]
        elif upper is None:
            upper = ref
        else:
            views += [(upper.at[n], ref.at[n]) for n in range(ref.shape[0])]
            upper = None
    return views


def gram_kernel(stacks, before, *refs):
    spans = panel_spans()
    pieces, refs = flat(refs[:stacks]), refs[stacks:]
    old, refs = (refs[: len(spans)], refs[len(spans) :]) if before else (None, refs)
    new, (columns, sems) = refs[: len(spans)], refs[len(spans) :]
    for copy in bring(pieces, columns, sems):
        copy.wait()
    for number, (low, size) in enumerate(spans):
        product = panel_product(columns, low, size)
        new[number][...] = product + old[number][...] if before else product


def gram_part(pieces, before=()):
    count = sum(piece.shape[0] * piece.shape[1] for piece in pieces) // FF
    inside = pl.BlockSpec(memory_space=pltpu.VMEM)
    return pl.pallas_call(
        lambda *refs: gram_kernel(len(pieces), bool(before), *refs),
        out_shape=[jax.ShapeDtypeStruct((FF - low, size), F32) for low, size in panel_spans()],
        in_specs=[pl.BlockSpec(memory_space=pl.ANY)] * len(pieces) + [inside] * len(before),
        out_specs=[inside] * len(panel_spans()),
        scratch_shapes=[pltpu.VMEM((FF, count * COLS), BF), pltpu.SemaphoreType.DMA((count, 2))],
        compiler_params=params(16),
        name="gram",
    )(*pieces, *before)


def newton_kernel(stacks, places, fresh_at, *refs):
    spans = panel_spans()
    pieces, refs = flat(refs[:stacks]), refs[stacks:]
    before, refs = refs[: len(spans)], refs[len(spans) :]
    own, rows_out, cols_out, whole, fresh, gram, sems, fresh_sems = refs
    early, late, core = place()
    floor = lax.axis_index("shard") // 2
    rep = block_of(early, late, core)
    fresh_copies = bring([pieces[number] for number in fresh_at], fresh, fresh_sems)
    copies = []
    for number, (k, j) in enumerate(places):
        block = block_of((early - k + SIDE) % SIDE, (late - j + SIDE) % SIDE, core)
        for part, piece in enumerate(pieces[number]):
            target = whole.at[pl.ds(part * HALF, HALF), block_columns(block)]
            copies.append(pltpu.make_async_copy(piece, target, sems.at[number, part]))
    for copy in copies:
        copy.start()
    start = own[...].astype(F32).T
    for copy in fresh_copies:
        copy.wait()
    squares = jnp.zeros((), F32)
    for number, (low, size) in enumerate(spans):
        panel = panel_product(fresh, low, size)
        panel = panel + before[number][...]
        on_line = lax.broadcasted_iota(jnp.int32, (size, size), 0) == lax.broadcasted_iota(
            jnp.int32, (size, size), 1
        )
        squares = squares + jnp.sum(jnp.where(on_line, panel[:size], 0.0))
        panel = panel.astype(BF)
        gram[low:, low : low + size] = panel
        if low + size < FF:
            gram[low : low + size, low + size :] = panel[size:].T
    factor = spectral_gain * math.sqrt(FF * D) / jnp.sqrt(jnp.full((1, 1), squares) + epsilon)
    scale = factor * factor / D
    half = rep % 2
    layer = (floor - rep // 4 + SIDE) % SIDE
    flipped = (rep // 2 % 2 + core) % 2
    base = layer * (2 * ROWS) + flipped * ROWS + half * (STRIP - 8)

    def strip_of(ref):
        window = ref[pl.ds(pl.multiple_of(base, 16), STRIP + 8), :].astype(F32)
        return jnp.where(half == 0, window[:STRIP], window[8:])

    first = scale * jnp.dot(start.astype(BF), gram[...], preferred_element_type=F32)
    strip = scale * strip_of(gram)
    power = jnp.concatenate([first, strip], axis=0)
    for _ in range(3):
        product = jnp.dot(power.astype(BF), gram[...], preferred_element_type=F32)
        power = 1.5 * power - (0.5 * scale) * product
    mixed = (0.75 * strip + 0.5 * power[COLS:]).astype(BF)
    for copy in copies:
        copy.wait()
    product = jnp.dot(mixed, whole[...], preferred_element_type=F32)
    rows_out[...] = (factor * (2.25 * strip_of(whole) - product)).astype(BF)
    columns = (factor * (2.25 * start - 0.75 * first - 0.5 * power[:COLS])).T.astype(BF)
    for k in range(SIDE):
        for i in range(2):
            at = ((floor - k + SIDE) % SIDE * 2 + (core + i) % 2) * ROWS
            low = (2 * k + i) * ROWS
            cols_out[pl.ds(pl.multiple_of(at, 16), ROWS), :] = columns[low : low + ROWS]


def newton(pieces, places, fresh_at, before, own):
    anywhere = pl.BlockSpec(memory_space=pl.ANY)
    inside = pl.BlockSpec(memory_space=pltpu.VMEM)
    return pl.pallas_call(
        lambda *refs: newton_kernel(len(pieces), places, fresh_at, *refs),
        out_shape=[jax.ShapeDtypeStruct((STRIP, D), BF), jax.ShapeDtypeStruct((FF, COLS), BF)],
        in_specs=[anywhere] * len(pieces) + [inside] * (len(before) + 1),
        out_specs=[inside, inside],
        scratch_shapes=[
            pltpu.VMEM((FF, D), BF),
            pltpu.VMEM((FF, len(fresh_at) * COLS), BF),
            pltpu.VMEM((FF, FF), BF),
            pltpu.SemaphoreType.DMA((16, 2)),
            pltpu.SemaphoreType.DMA((len(fresh_at), 2)),
        ],
        compiler_params=params(24),
        name="newton",
    )(*pieces, *before, own)


def slots_of(owner, who):
    mine = owner == who
    count = jnp.sum(mine.astype(jnp.int32))
    index = jnp.arange(MATS, dtype=jnp.int32)
    first = jnp.min(jnp.where(mine, index, MATS))
    last = jnp.max(jnp.where(mine, index, -1))
    return (jnp.where(count > 0, first, 0), count > 0), (jnp.where(count > 1, last, 0), count > 1)


def choose_kernel(choice, *refs):
    pieces, out = refs[:-1], refs[-1]
    for slot in range(CAP):
        for number, piece in enumerate(pieces):

            @pl.when(choice[slot] == number)
            def _():
                out[0, slot] = piece[...] if len(piece.shape) == 2 else piece[0, slot]

        @pl.when(choice[slot] == len(pieces))
        def _():
            out[0, slot] = jnp.zeros((STRIP, D), BF)


def choose(choice, pieces):
    inside = pl.BlockSpec(memory_space=pltpu.VMEM)
    return pl.pallas_call(
        choose_kernel,
        out_shape=jax.ShapeDtypeStruct((1, CAP, STRIP, D), BF),
        in_specs=[pl.BlockSpec(memory_space=pltpu.SMEM)] + [inside] * len(pieces),
        out_specs=inside,
        compiler_params=params(6),
        name="choose",
    )(jnp.stack(choice).astype(jnp.int32), *pieces)


def per_device(grads, momentum, owner):
    grads = grads[0]
    axes = ("rep", "shard")

    def move(piece, phase, step):
        return lax.ppermute(piece, axes, along(phase, step))

    def cut(*wanted):
        return split(grads, [[(early, late) for late in lates] for early, lates in wanted])

    one, two = (3, 0), (2, 1)
    across_one, across_two = cut((2, one), (2, two))
    across_one, across_two = move(across_one, 0, 1), move(across_two, 0, 3)
    side_one, side_two = cut((3, one), (1, two))
    side_two, side_one = move(side_two, 0, 1), move(side_one, 0, 3)
    next_one, next_two = cut((1, one), (3, two))
    mine_one, mine_two = cut((0, one), (0, two))
    relay_one = move(add(next_one, across_one).astype(BF), 0, 1)
    relay_two = move(add(next_two, across_two).astype(BF), 0, 3)
    late_2 = move(add(mine_two[0], relay_two[0], side_two[0]).astype(BF), 1, 2)
    late_1 = move(add(mine_two[1], relay_two[1], side_two[1]).astype(BF), 1, 1)
    late_3 = move(add(mine_one[0], relay_one[0], side_one[0]).astype(BF), 1, 3)
    terms = (mine_one[1], relay_one[1], side_one[1], late_2, late_1, late_3)
    summed = add(*terms)
    rounded = (summed + decay_rate * (decay_rate * momentum + summed)).astype(BF)
    shard = lax.axis_index("shard")
    floor, core = shard // 2, shard % 2
    swap = [(s, s ^ 1) for s in range(8)]
    by_core = rounded.reshape(SIDE, 2, ROWS, COLS)
    mine = lax.dynamic_index_in_dim(by_core, core, 1, keepdims=False)
    theirs = lax.dynamic_index_in_dim(by_core, 1 - core, 1, keepdims=False)
    layers = jnp.stack([mine, lax.ppermute(theirs, "shard", swap)], axis=1)

    def layer(step):
        return lax.dynamic_index_in_dim(layers, (floor + step) % SIDE, 0, keepdims=False)

    parts = [layer(0)] + [lax.ppermute(layer(n), "shard", along_z(n)) for n in (1, 2, 3)]
    own = jnp.stack(parts).reshape(FF, COLS)
    line = jnp.stack([own, move(own, 0, 1), move(own, 0, 3), move(own, 0, 2)])
    halves = [line[:, :HALF], line[:, HALF:]]
    aheads, behinds = [move(half, 1, 1) for half in halves], [move(half, 1, 3) for half in halves]
    terms, _ = lax.optimization_barrier((terms, line))
    new_momentum = decay_rate * momentum + add(*terms)
    gram = gram_part([line])
    aheads[1], behinds[1], gram, new_momentum = lax.optimization_barrier((aheads[1], behinds[1], gram, new_momentum))
    across_as = [move(ahead[:2], 1, 1) for ahead in aheads]
    across_bs = [move(behind[2:], 1, 3) for behind in behinds]
    gram = gram_part([*aheads, *behinds], gram)
    pieces = [line, *aheads, *behinds, *across_as, *across_bs]
    places = [(k, j) for j in (0, 1, 3, 2) for k in (0, 1, 3, 2)]
    strip, columns = newton(pieces, places, (12, 13, 14, 15), gram, own)
    pieces = [strip] + [lax.ppermute(strip, "shard", along_z(n)) for n in (1, 2, 3)]
    update = lax.all_to_all(columns.reshape(MATS, ROWS, COLS), "shard", 0, 0, tiled=True)
    pieces, update = lax.optimization_barrier((pieces, update))
    wanted = [(floor - m // 2 + 4) % 4 for m, _ in slots_of(owner, floor * 2 + 1 - core)]
    handed = lax.ppermute(choose(wanted, pieces), "shard", swap)
    choice = []
    for m, filled in slots_of(owner, shard):
        choice.append(jnp.where(filled, jnp.where(m % 2 == core, (floor - m // 2 + 4) % 4, 4), 5))
    return new_momentum, update, choose(choice, [*pieces, handed])


def solution(mesh):
    placed = (P("rep", None, "shard", None), P(None, "shard", "rep"), P())
    return jax.shard_map(
        per_device,
        mesh=mesh,
        in_specs=placed,
        out_specs=(P(None, "shard", "rep"), P(None, "shard", "rep"), P("shard", None, "rep", None)),
        check_vma=False,
    )
```

```python
import math

import jax
import jax.numpy as jnp
from jax import lax
from jax.experimental import pallas as pl
from jax.experimental.pallas import tpu as pltpu
from jax.sharding import PartitionSpec as P

D = 2048
FF = 1408
CAP = 2
MATS = 8
SIDE = 4
ROWS = FF // 8
COLS = D // 16
STRIP = FF // 16
HALF = FF // 2
PANEL = 256

decay_rate = 0.95
spectral_gain = 0.75
epsilon = 1e-06

BF = jnp.bfloat16
F32 = jnp.float32


def along_z(step):
    return [(z * 2 + c, (z + step) % 4 * 2 + c) for z in range(4) for c in range(2)]


def along(phase, step):
    pairs = []
    for y in range(SIDE):
        for x in range(SIDE):
            for shard in range(8):
                to_x = (x + step) % SIDE if shard % 2 == phase else x
                to_y = y if shard % 2 == phase else (y + step) % SIDE
                pairs.append(((y * SIDE + x) * 8 + shard, (to_y * SIDE + to_x) * 8 + shard))
    return pairs


def place():
    rep = lax.axis_index("rep")
    y, x = rep // SIDE, rep % SIDE
    core = lax.axis_index("shard") % 2
    return jnp.where(core == 0, x, y), jnp.where(core == 0, y, x), core


def block_of(early, late, core):
    return jnp.where(core == 0, late * SIDE + early, early * SIDE + late)


def params(mebibytes):
    return pltpu.CompilerParams(vmem_limit_bytes=mebibytes * 1024 * 1024)


def block_columns(block):
    return pl.ds(pl.multiple_of(block * COLS, COLS), COLS)


def split_kernel(wanted, grads, *refs):
    outs, sems = refs[:-1], refs[-1]
    early, late, core = place()
    copies = []
    for out, steps in zip(outs, wanted):
        for number, (early_step, late_step) in enumerate(steps):
            block = block_of((early + early_step) % SIDE, (late + late_step) % SIDE, core)
            source = grads.at[:, :, block_columns(block)]
            copies.append(pltpu.make_async_copy(source, out.at[number], sems.at[len(copies)]))
    for copy in copies:
        copy.start()
    for copy in copies:
        copy.wait()


def split(grads, wanted, mebibytes):
    return pl.pallas_call(
        lambda *refs: split_kernel(wanted, *refs),
        out_shape=[jax.ShapeDtypeStruct((len(steps), MATS, ROWS, COLS), BF) for steps in wanted],
        in_specs=[pl.BlockSpec(memory_space=pl.ANY)],
        out_specs=[pl.BlockSpec(memory_space=pltpu.VMEM)] * len(wanted),
        scratch_shapes=[pltpu.SemaphoreType.DMA((sum(len(steps) for steps in wanted),))],
        compiler_params=params(mebibytes),
        name="split",
    )(grads)


def add(*parts):
    total = parts[0].astype(F32)
    for part in parts[1:]:
        total = total + part.astype(F32)
    return total


def panel_spans():
    return [(low, min(PANEL, FF - low)) for low in range(0, FF, PANEL)]


def panel_product(columns, low, size):
    return lax.dot_general(
        columns[low:, :], columns[low : low + size, :], (((1,), (1,)), ((), ())), preferred_element_type=F32
    )


def bring(pieces, columns, sems):
    copies = []
    for number, halves in enumerate(pieces):
        for half, piece in enumerate(halves):
            target = columns.at[pl.ds(half * HALF, HALF), pl.ds(number * COLS, COLS)]
            copies.append(pltpu.make_async_copy(piece, target, sems.at[number, half]))
    for copy in copies:
        copy.start()
    return copies


def flat(refs):
    views, upper = [], None
    for ref in refs:
        if ref.shape[1] == FF:
            views += [tuple(ref.at[n, pl.ds(half * HALF, HALF)] for half in range(2)) for n in range(ref.shape[0])]
        elif upper is None:
            upper = ref
        else:
            views += [(upper.at[n], ref.at[n]) for n in range(ref.shape[0])]
            upper = None
    return views


def gram_kernel(stacks, before, *refs):
    spans = panel_spans()
    pieces, refs = flat(refs[:stacks]), refs[stacks:]
    old, refs = (refs[: len(spans)], refs[len(spans) :]) if before else (None, refs)
    new, (columns, sems) = refs[: len(spans)], refs[len(spans) :]
    for copy in bring(pieces, columns, sems):
        copy.wait()
    for number, (low, size) in enumerate(spans):
        product = panel_product(columns, low, size)
        new[number][...] = product + old[number][...] if before else product


def gram_part(pieces, before=()):
    count = sum(piece.shape[0] * piece.shape[1] for piece in pieces) // FF
    inside = pl.BlockSpec(memory_space=pltpu.VMEM)
    return pl.pallas_call(
        lambda *refs: gram_kernel(len(pieces), bool(before), *refs),
        out_shape=[jax.ShapeDtypeStruct((FF - low, size), F32) for low, size in panel_spans()],
        in_specs=[pl.BlockSpec(memory_space=pl.ANY)] * len(pieces) + [inside] * len(before),
        out_specs=[inside] * len(panel_spans()),
        scratch_shapes=[pltpu.VMEM((FF, count * COLS), BF), pltpu.SemaphoreType.DMA((count, 2))],
        compiler_params=params(16),
        name="gram",
    )(*pieces, *before)


def newton_kernel(stacks, places, fresh_at, *refs):
    spans = panel_spans()
    pieces, refs = flat(refs[:stacks]), refs[stacks:]
    before, refs = refs[: len(spans)], refs[len(spans) :]
    own, rows_out, cols_out, whole, fresh, gram, sems, fresh_sems = refs
    early, late, core = place()
    floor = lax.axis_index("shard") // 2
    rep = block_of(early, late, core)
    fresh_copies = bring([pieces[number] for number in fresh_at], fresh, fresh_sems)
    copies = []
    for number, (k, j) in enumerate(places):
        block = block_of((early - k + SIDE) % SIDE, (late - j + SIDE) % SIDE, core)
        for part, piece in enumerate(pieces[number]):
            target = whole.at[pl.ds(part * HALF, HALF), block_columns(block)]
            copies.append(pltpu.make_async_copy(piece, target, sems.at[number, part]))
    for copy in copies:
        copy.start()
    start = own[...].astype(F32).T
    for copy in fresh_copies:
        copy.wait()
    squares = jnp.zeros((), F32)
    for number, (low, size) in enumerate(spans):
        panel = panel_product(fresh, low, size)
        panel = panel + before[number][...]
        on_line = lax.broadcasted_iota(jnp.int32, (size, size), 0) == lax.broadcasted_iota(
            jnp.int32, (size, size), 1
        )
        squares = squares + jnp.sum(jnp.where(on_line, panel[:size], 0.0))
        panel = panel.astype(BF)
        gram[low:, low : low + size] = panel
        if low + size < FF:
            gram[low : low + size, low + size :] = panel[size:].T
    factor = spectral_gain * math.sqrt(FF * D) / jnp.sqrt(jnp.full((1, 1), squares) + epsilon)
    scale = factor * factor / D
    half = rep % 2
    layer = (floor - rep // 4 + SIDE) % SIDE
    flipped = (rep // 2 % 2 + core) % 2
    base = layer * (2 * ROWS) + flipped * ROWS + half * (STRIP - 8)

    def strip_of(ref):
        window = ref[pl.ds(pl.multiple_of(base, 16), STRIP + 8), :].astype(F32)
        return jnp.where(half == 0, window[:STRIP], window[8:])

    first = scale * jnp.dot(start.astype(BF), gram[...], preferred_element_type=F32)
    strip = scale * strip_of(gram)
    power = jnp.concatenate([first, strip], axis=0)
    for _ in range(3):
        product = jnp.dot(power.astype(BF), gram[...], preferred_element_type=F32)
        power = 1.5 * power - (0.5 * scale) * product
    mixed = (0.75 * strip + 0.5 * power[COLS:]).astype(BF)
    for copy in copies:
        copy.wait()
    product = jnp.dot(mixed, whole[...], preferred_element_type=F32)
    rows_out[...] = (factor * (2.25 * strip_of(whole) - product)).astype(BF)
    columns = (factor * (2.25 * start - 0.75 * first - 0.5 * power[:COLS])).T.astype(BF)
    for k in range(SIDE):
        for i in range(2):
            at = ((floor - k + SIDE) % SIDE * 2 + (core + i) % 2) * ROWS
            low = (2 * k + i) * ROWS
            cols_out[pl.ds(pl.multiple_of(at, 16), ROWS), :] = columns[low : low + ROWS]


def newton(pieces, places, fresh_at, before, own):
    anywhere = pl.BlockSpec(memory_space=pl.ANY)
    inside = pl.BlockSpec(memory_space=pltpu.VMEM)
    return pl.pallas_call(
        lambda *refs: newton_kernel(len(pieces), places, fresh_at, *refs),
        out_shape=[jax.ShapeDtypeStruct((STRIP, D), BF), jax.ShapeDtypeStruct((FF, COLS), BF)],
        in_specs=[anywhere] * len(pieces) + [inside] * (len(before) + 1),
        out_specs=[inside, inside],
        scratch_shapes=[
            pltpu.VMEM((FF, D), BF),
            pltpu.VMEM((FF, len(fresh_at) * COLS), BF),
            pltpu.VMEM((FF, FF), BF),
            pltpu.SemaphoreType.DMA((16, 2)),
            pltpu.SemaphoreType.DMA((len(fresh_at), 2)),
        ],
        compiler_params=params(24),
        name="newton",
    )(*pieces, *before, own)


def slots_of(owner, who):
    mine = owner == who
    count = jnp.sum(mine.astype(jnp.int32))
    index = jnp.arange(MATS, dtype=jnp.int32)
    first = jnp.min(jnp.where(mine, index, MATS))
    last = jnp.max(jnp.where(mine, index, -1))
    return (jnp.where(count > 0, first, 0), count > 0), (jnp.where(count > 1, last, 0), count > 1)


def choose_kernel(count, choice, *refs):
    pieces, rest = refs[:count], refs[count:]
    out = rest[len(rest) // 2]
    if len(rest) == 3:
        rest[2][...] = rest[0][...]
    for slot in range(CAP):
        for number, piece in enumerate(pieces):

            @pl.when(choice[slot] == number)
            def _():
                out[0, slot] = piece[...] if len(piece.shape) == 2 else piece[0, slot]

        @pl.when(choice[slot] == count)
        def _():
            out[0, slot] = jnp.zeros((STRIP, D), BF)


def choose(choice, pieces, *along):
    inside = pl.BlockSpec(memory_space=pltpu.VMEM)
    return pl.pallas_call(
        lambda *refs: choose_kernel(len(pieces), *refs),
        out_shape=[
            jax.ShapeDtypeStruct((1, CAP, STRIP, D), BF),
            *[jax.ShapeDtypeStruct(array.shape, array.dtype) for array in along],
        ],
        in_specs=[pl.BlockSpec(memory_space=pltpu.SMEM)] + [inside] * (len(pieces) + len(along)),
        out_specs=[inside] * (1 + len(along)),
        compiler_params=params(6),
        name="choose",
    )(jnp.stack(choice).astype(jnp.int32), *pieces, *along)


def per_device(grads, momentum, owner):
    grads = grads[0]
    axes = ("rep", "shard")

    def move(piece, phase, step):
        return lax.ppermute(piece, axes, along(phase, step))

    def cut(*wanted, mebibytes=4):
        return split(grads, [[(early, late) for late in lates] for early, lates in wanted], mebibytes)

    one, two = (3, 0), (2, 1)
    across_one, across_two = cut((2, one), (2, two), mebibytes=58)
    across_one, across_two = move(across_one, 0, 1), move(across_two, 0, 3)
    side_one, side_two = cut((3, one), (1, two))
    side_two, side_one = move(side_two, 0, 1), move(side_one, 0, 3)
    next_one, next_two = cut((1, one), (3, two))
    mine_one, mine_two = cut((0, one), (0, two))
    relay_one = move(add(next_one, across_one).astype(BF), 0, 1)
    relay_two = move(add(next_two, across_two).astype(BF), 0, 3)
    sums = [add(mine_two[n], relay_two[n], side_two[n]).astype(BF) for n in range(2)]
    sums.append(add(mine_one[0], relay_one[0], side_one[0]).astype(BF))
    sum_2, sum_1, sum_3 = lax.optimization_barrier(sums)
    late_2, late_1, late_3 = move(sum_2, 1, 2), move(sum_1, 1, 1), move(sum_3, 1, 3)
    terms = (mine_one[1], relay_one[1], side_one[1], late_2, late_1, late_3)
    summed = add(*terms)
    rounded = (summed + decay_rate * (decay_rate * momentum + summed)).astype(BF)
    shard = lax.axis_index("shard")
    floor, core = shard // 2, shard % 2
    swap = [(s, s ^ 1) for s in range(8)]
    by_core = rounded.reshape(SIDE, 2, ROWS, COLS)
    mine = lax.dynamic_index_in_dim(by_core, core, 1, keepdims=False)
    theirs = lax.dynamic_index_in_dim(by_core, 1 - core, 1, keepdims=False)
    layers = jnp.stack([mine, lax.ppermute(theirs, "shard", swap)], axis=1)

    def layer(step):
        return lax.dynamic_index_in_dim(layers, (floor + step) % SIDE, 0, keepdims=False)

    part_2, part_1, part_3 = [lax.ppermute(layer(n), "shard", along_z(n)) for n in (2, 1, 3)]
    own = jnp.stack([layer(0), part_1, part_2, part_3]).reshape(FF, COLS)
    line_2, line_1, line_3 = move(own, 0, 2), move(own, 0, 1), move(own, 0, 3)
    line = jnp.stack([own, line_1, line_3, line_2])
    halves = [line[:, :HALF], line[:, HALF:]]
    aheads, behinds = [move(half, 1, 1) for half in halves], [move(half, 1, 3) for half in halves]
    terms, _ = lax.optimization_barrier((terms, line))
    new_momentum = decay_rate * momentum + add(*terms)
    gram = gram_part([line])
    aheads[1], behinds[1], gram, new_momentum = lax.optimization_barrier((aheads[1], behinds[1], gram, new_momentum))
    across_as = [move(ahead[:2], 1, 1) for ahead in aheads]
    across_bs = [move(behind[2:], 1, 3) for behind in behinds]
    gram = gram_part([*aheads, *behinds], gram)
    pieces = [line, *aheads, *behinds, *across_as, *across_bs]
    places = [(k, j) for j in (0, 1, 3, 2) for k in (0, 1, 3, 2)]
    strip, columns = newton(pieces, places, (12, 13, 14, 15), gram, own)
    strip_2, strip_1, strip_3 = [lax.ppermute(strip, "shard", along_z(n)) for n in (2, 1, 3)]
    pieces = [strip, strip_1, strip_2, strip_3]
    update = lax.all_to_all(columns.reshape(MATS, ROWS, COLS), "shard", 0, 0, tiled=True)
    pieces, update = lax.optimization_barrier((pieces, update))
    wanted = [(floor - m // 2 + 4) % 4 for m, _ in slots_of(owner, floor * 2 + 1 - core)]
    handed = lax.ppermute(choose(wanted, pieces)[0], "shard", swap)
    choice = []
    for m, filled in slots_of(owner, shard):
        choice.append(jnp.where(filled, jnp.where(m % 2 == core, (floor - m // 2 + 4) % 4, 4), 5))
    owned, update = choose(choice, [*pieces, handed], update)
    return new_momentum, update, owned


def solution(mesh):
    placed = (P("rep", None, "shard", None), P(None, "shard", "rep"), P())
    return jax.shard_map(
        per_device,
        mesh=mesh,
        in_specs=placed,
        out_specs=(P(None, "shard", "rep"), P(None, "shard", "rep"), P("shard", None, "rep", None)),
        check_vma=False,
    )
```

```python
import math

import jax
import jax.numpy as jnp
from jax import lax
from jax.experimental import pallas as pl
from jax.experimental.pallas import tpu as pltpu
from jax.sharding import PartitionSpec as P

D = 2048
FF = 1408
CAP = 2
MATS = 8
SIDE = 4
ROWS = FF // 8
COLS = D // 16
STRIP = FF // 16
HALF = FF // 2
PANEL = 256

decay_rate = 0.95
spectral_gain = 0.75
epsilon = 1e-06

BF = jnp.bfloat16
F32 = jnp.float32


def along_z(step):
    return [(z * 2 + c, (z + step) % 4 * 2 + c) for z in range(4) for c in range(2)]


def along(phase, step):
    pairs = []
    for y in range(SIDE):
        for x in range(SIDE):
            for shard in range(8):
                to_x = (x + step) % SIDE if shard % 2 == phase else x
                to_y = y if shard % 2 == phase else (y + step) % SIDE
                pairs.append(((y * SIDE + x) * 8 + shard, (to_y * SIDE + to_x) * 8 + shard))
    return pairs


def place():
    rep = lax.axis_index("rep")
    y, x = rep // SIDE, rep % SIDE
    core = lax.axis_index("shard") % 2
    return jnp.where(core == 0, x, y), jnp.where(core == 0, y, x), core


def block_of(early, late, core):
    return jnp.where(core == 0, late * SIDE + early, early * SIDE + late)


def params(mebibytes):
    return pltpu.CompilerParams(vmem_limit_bytes=mebibytes * 1024 * 1024)


def block_columns(block):
    return pl.ds(pl.multiple_of(block * COLS, COLS), COLS)


def split_kernel(wanted, grads, *refs):
    outs, sems = refs[:-1], refs[-1]
    early, late, core = place()
    copies = []
    for out, steps in zip(outs, wanted):
        for number, (early_step, late_step) in enumerate(steps):
            block = block_of((early + early_step) % SIDE, (late + late_step) % SIDE, core)
            source = grads.at[:, :, block_columns(block)]
            copies.append(pltpu.make_async_copy(source, out.at[number], sems.at[len(copies)]))
    for copy in copies:
        copy.start()
    for copy in copies:
        copy.wait()


def split(grads, wanted, mebibytes):
    return pl.pallas_call(
        lambda *refs: split_kernel(wanted, *refs),
        out_shape=[jax.ShapeDtypeStruct((len(steps), MATS, ROWS, COLS), BF) for steps in wanted],
        in_specs=[pl.BlockSpec(memory_space=pl.ANY)],
        out_specs=[pl.BlockSpec(memory_space=pltpu.VMEM)] * len(wanted),
        scratch_shapes=[pltpu.SemaphoreType.DMA((sum(len(steps) for steps in wanted),))],
        compiler_params=params(mebibytes),
        name="split",
    )(grads)


def add(*parts):
    total = parts[0].astype(F32)
    for part in parts[1:]:
        total = total + part.astype(F32)
    return total


def panel_spans():
    return [(low, min(PANEL, FF - low)) for low in range(0, FF, PANEL)]


def panel_product(columns, low, size):
    return lax.dot_general(
        columns[low:, :], columns[low : low + size, :], (((1,), (1,)), ((), ())), preferred_element_type=F32
    )


def bring(pieces, columns, sems):
    copies = []
    for number, halves in enumerate(pieces):
        for half, piece in enumerate(halves):
            target = columns.at[pl.ds(half * HALF, HALF), pl.ds(number * COLS, COLS)]
            copies.append(pltpu.make_async_copy(piece, target, sems.at[number, half]))
    for copy in copies:
        copy.start()
    return copies


def flat(refs):
    views, upper = [], None
    for ref in refs:
        if ref.shape[1] == FF:
            views += [tuple(ref.at[n, pl.ds(half * HALF, HALF)] for half in range(2)) for n in range(ref.shape[0])]
        elif upper is None:
            upper = ref
        else:
            views += [(upper.at[n], ref.at[n]) for n in range(ref.shape[0])]
            upper = None
    return views


def gram_kernel(stacks, before, *refs):
    spans = panel_spans()
    pieces, refs = flat(refs[:stacks]), refs[stacks:]
    old, refs = (refs[: len(spans)], refs[len(spans) :]) if before else (None, refs)
    new, (columns, sems) = refs[: len(spans)], refs[len(spans) :]
    for copy in bring(pieces, columns, sems):
        copy.wait()
    for number, (low, size) in enumerate(spans):
        product = panel_product(columns, low, size)
        new[number][...] = product + old[number][...] if before else product


def gram_part(pieces, before=()):
    count = sum(piece.shape[0] * piece.shape[1] for piece in pieces) // FF
    inside = pl.BlockSpec(memory_space=pltpu.VMEM)
    return pl.pallas_call(
        lambda *refs: gram_kernel(len(pieces), bool(before), *refs),
        out_shape=[jax.ShapeDtypeStruct((FF - low, size), F32) for low, size in panel_spans()],
        in_specs=[pl.BlockSpec(memory_space=pl.ANY)] * len(pieces) + [inside] * len(before),
        out_specs=[inside] * len(panel_spans()),
        scratch_shapes=[pltpu.VMEM((FF, count * COLS), BF), pltpu.SemaphoreType.DMA((count, 2))],
        compiler_params=params(16),
        name="gram",
    )(*pieces, *before)


def newton_kernel(stacks, places, fresh_at, *refs):
    spans = panel_spans()
    pieces, refs = flat(refs[:stacks]), refs[stacks:]
    before, refs = refs[: len(spans)], refs[len(spans) :]
    own, rows_out, cols_out, whole, fresh, gram, sems, fresh_sems = refs
    early, late, core = place()
    floor = lax.axis_index("shard") // 2
    rep = block_of(early, late, core)
    fresh_copies = bring([pieces[number] for number in fresh_at], fresh, fresh_sems)
    copies = []
    for number, (k, j) in enumerate(places):
        block = block_of((early - k + SIDE) % SIDE, (late - j + SIDE) % SIDE, core)
        for part, piece in enumerate(pieces[number]):
            target = whole.at[pl.ds(part * HALF, HALF), block_columns(block)]
            copies.append(pltpu.make_async_copy(piece, target, sems.at[number, part]))
    for copy in copies:
        copy.start()
    start = own[...].astype(F32).T
    for copy in fresh_copies:
        copy.wait()
    squares = jnp.zeros((), F32)
    for number, (low, size) in enumerate(spans):
        panel = panel_product(fresh, low, size)
        panel = panel + before[number][...]
        on_line = lax.broadcasted_iota(jnp.int32, (size, size), 0) == lax.broadcasted_iota(
            jnp.int32, (size, size), 1
        )
        squares = squares + jnp.sum(jnp.where(on_line, panel[:size], 0.0))
        panel = panel.astype(BF)
        gram[low:, low : low + size] = panel
        if low + size < FF:
            gram[low : low + size, low + size :] = panel[size:].T
    factor = spectral_gain * math.sqrt(FF * D) / jnp.sqrt(jnp.full((1, 1), squares) + epsilon)
    scale = factor * factor / D
    half = rep % 2
    layer = (floor - rep // 4 + SIDE) % SIDE
    flipped = (rep // 2 % 2 + core) % 2
    base = layer * (2 * ROWS) + flipped * ROWS + half * (STRIP - 8)

    def strip_of(ref):
        window = ref[pl.ds(pl.multiple_of(base, 16), STRIP + 8), :].astype(F32)
        return jnp.where(half == 0, window[:STRIP], window[8:])

    first = scale * jnp.dot(start.astype(BF), gram[...], preferred_element_type=F32)
    strip = scale * strip_of(gram)
    power = jnp.concatenate([first, strip], axis=0)
    for _ in range(3):
        product = jnp.dot(power.astype(BF), gram[...], preferred_element_type=F32)
        power = 1.5 * power - (0.5 * scale) * product
    mixed = (0.75 * strip + 0.5 * power[COLS:]).astype(BF)
    for copy in copies:
        copy.wait()
    product = jnp.dot(mixed, whole[...], preferred_element_type=F32)
    rows_out[...] = (factor * (2.25 * strip_of(whole) - product)).astype(BF)
    columns = (factor * (2.25 * start - 0.75 * first - 0.5 * power[:COLS])).T.astype(BF)
    for k in range(SIDE):
        for i in range(2):
            at = ((floor - k + SIDE) % SIDE * 2 + (core + i) % 2) * ROWS
            low = (2 * k + i) * ROWS
            cols_out[pl.ds(pl.multiple_of(at, 16), ROWS), :] = columns[low : low + ROWS]


def newton(pieces, places, fresh_at, before, own):
    anywhere = pl.BlockSpec(memory_space=pl.ANY)
    inside = pl.BlockSpec(memory_space=pltpu.VMEM)
    return pl.pallas_call(
        lambda *refs: newton_kernel(len(pieces), places, fresh_at, *refs),
        out_shape=[jax.ShapeDtypeStruct((STRIP, D), BF), jax.ShapeDtypeStruct((FF, COLS), BF)],
        in_specs=[anywhere] * len(pieces) + [inside] * (len(before) + 1),
        out_specs=[inside, inside],
        scratch_shapes=[
            pltpu.VMEM((FF, D), BF),
            pltpu.VMEM((FF, len(fresh_at) * COLS), BF),
            pltpu.VMEM((FF, FF), BF),
            pltpu.SemaphoreType.DMA((16, 2)),
            pltpu.SemaphoreType.DMA((len(fresh_at), 2)),
        ],
        compiler_params=params(24),
        name="newton",
    )(*pieces, *before, own)


def slots_of(owner, who):
    mine = owner == who
    count = jnp.sum(mine.astype(jnp.int32))
    index = jnp.arange(MATS, dtype=jnp.int32)
    first = jnp.min(jnp.where(mine, index, MATS))
    last = jnp.max(jnp.where(mine, index, -1))
    return (jnp.where(count > 0, first, 0), count > 0), (jnp.where(count > 1, last, 0), count > 1)


def choose_kernel(count, choice, *refs):
    pieces, rest = refs[:count], refs[count:]
    out = rest[len(rest) // 2]
    if len(rest) == 3:
        rest[2][...] = rest[0][...]
    for slot in range(CAP):
        for number, piece in enumerate(pieces):

            @pl.when(choice[slot] == number)
            def _():
                out[0, slot] = piece[...] if len(piece.shape) == 2 else piece[0, slot]

        @pl.when(choice[slot] == count)
        def _():
            out[0, slot] = jnp.zeros((STRIP, D), BF)


def choose(choice, pieces, *along):
    inside = pl.BlockSpec(memory_space=pltpu.VMEM)
    return pl.pallas_call(
        lambda *refs: choose_kernel(len(pieces), *refs),
        out_shape=[
            jax.ShapeDtypeStruct((1, CAP, STRIP, D), BF),
            *[jax.ShapeDtypeStruct(array.shape, array.dtype) for array in along],
        ],
        in_specs=[pl.BlockSpec(memory_space=pltpu.SMEM)] + [inside] * (len(pieces) + len(along)),
        out_specs=[inside] * (1 + len(along)),
        compiler_params=params(6),
        name="choose",
    )(jnp.stack(choice).astype(jnp.int32), *pieces, *along)


def per_device(grads, momentum, owner):
    grads = grads[0]
    axes = ("rep", "shard")

    def move(piece, phase, step):
        return lax.ppermute(piece, axes, along(phase, step))

    def cut(*wanted, mebibytes=4):
        return split(grads, [[(early, late) for late in lates] for early, lates in wanted], mebibytes)

    one, two = (3, 0), (2, 1)
    across_one, across_two = cut((2, one), (2, two), mebibytes=58)
    across_one, across_two = move(across_one, 0, 1), move(across_two, 0, 3)
    side_one, side_two = cut((3, one), (1, two))
    side_two, side_one = move(side_two, 0, 1), move(side_one, 0, 3)
    next_one, next_two = cut((1, one), (3, two))
    mine_one, mine_two = cut((0, one), (0, two))
    relay_one = move(add(next_one, across_one).astype(BF), 0, 1)
    relay_two = move(add(next_two, across_two).astype(BF), 0, 3)
    sums = [add(mine_two[n], relay_two[n], side_two[n]).astype(BF) for n in range(2)]
    sums.append(add(mine_one[0], relay_one[0], side_one[0]).astype(BF))
    sum_2, sum_1, sum_3 = lax.optimization_barrier(sums)
    late_2, late_1, late_3 = move(sum_2, 1, 2), move(sum_1, 1, 1), move(sum_3, 1, 3)
    terms = (mine_one[1], relay_one[1], side_one[1], late_2, late_1, late_3)
    summed = add(*terms)
    rounded = (summed + decay_rate * (decay_rate * momentum + summed)).astype(BF)
    shard = lax.axis_index("shard")
    floor, core = shard // 2, shard % 2
    swap = [(s, s ^ 1) for s in range(8)]
    by_core = rounded.reshape(SIDE, 2, ROWS, COLS)
    mine = lax.dynamic_index_in_dim(by_core, core, 1, keepdims=False)
    theirs = lax.dynamic_index_in_dim(by_core, 1 - core, 1, keepdims=False)
    layers = jnp.stack([mine, lax.ppermute(theirs, "shard", swap)], axis=1)

    def layer(step):
        return lax.dynamic_index_in_dim(layers, (floor + step) % SIDE, 0, keepdims=False)

    part_2, part_1, part_3 = [lax.ppermute(layer(n), "shard", along_z(n)) for n in (2, 1, 3)]
    own = jnp.stack([layer(0), part_1, part_2, part_3]).reshape(FF, COLS)
    line_1, line_3, line_2 = move(own, 0, 1), move(own, 0, 3), move(own, 0, 2)
    line = jnp.stack([own, line_1, line_3, line_2])
    halves = [line[:, :HALF], line[:, HALF:]]
    aheads, behinds = [move(half, 1, 1) for half in halves], [move(half, 1, 3) for half in halves]
    terms, _ = lax.optimization_barrier((terms, line))
    new_momentum = decay_rate * momentum + add(*terms)
    gram = gram_part([line])
    aheads[1], behinds[1], gram, new_momentum = lax.optimization_barrier((aheads[1], behinds[1], gram, new_momentum))
    across_as = [move(ahead[:2], 1, 1) for ahead in aheads]
    across_bs = [move(behind[2:], 1, 3) for behind in behinds]
    gram = gram_part([*aheads, *behinds], gram)
    pieces = [line, *aheads, *behinds, *across_as, *across_bs]
    places = [(k, j) for j in (0, 1, 3, 2) for k in (0, 1, 3, 2)]
    strip, columns = newton(pieces, places, (12, 13, 14, 15), gram, own)
    strip_2, strip_1, strip_3 = [lax.ppermute(strip, "shard", along_z(n)) for n in (2, 1, 3)]
    pieces = [strip, strip_1, strip_2, strip_3]
    update = lax.all_to_all(columns.reshape(MATS, ROWS, COLS), "shard", 0, 0, tiled=True)
    pieces, update = lax.optimization_barrier((pieces, update))
    wanted = [(floor - m // 2 + 4) % 4 for m, _ in slots_of(owner, floor * 2 + 1 - core)]
    handed = lax.ppermute(choose(wanted, pieces)[0], "shard", swap)
    choice = []
    for m, filled in slots_of(owner, shard):
        choice.append(jnp.where(filled, jnp.where(m % 2 == core, (floor - m // 2 + 4) % 4, 4), 5))
    owned, update = choose(choice, [*pieces, handed], update)
    return new_momentum, update, owned


def solution(mesh):
    placed = (P("rep", None, "shard", None), P(None, "shard", "rep"), P())
    return jax.shard_map(
        per_device,
        mesh=mesh,
        in_specs=placed,
        out_specs=(P(None, "shard", "rep"), P(None, "shard", "rep"), P("shard", None, "rep", None)),
        check_vma=False,
    )
```

```python
import math

import jax
import jax.numpy as jnp
from jax import lax
from jax.experimental import pallas as pl
from jax.experimental.pallas import tpu as pltpu
from jax.sharding import PartitionSpec as P

D = 2048
FF = 1408
CAP = 2
MATS = 8
SIDE = 4
ROWS = FF // 8
COLS = D // 16
STRIP = FF // 16
HALF = FF // 2
PANEL = 256

decay_rate = 0.95
spectral_gain = 0.75
epsilon = 1e-06

BF = jnp.bfloat16
F32 = jnp.float32


def along_z(step):
    return [(z * 2 + c, (z + step) % 4 * 2 + c) for z in range(4) for c in range(2)]


def along(phase, step):
    pairs = []
    for y in range(SIDE):
        for x in range(SIDE):
            for shard in range(8):
                to_x = (x + step) % SIDE if shard % 2 == phase else x
                to_y = y if shard % 2 == phase else (y + step) % SIDE
                pairs.append(((y * SIDE + x) * 8 + shard, (to_y * SIDE + to_x) * 8 + shard))
    return pairs


def place():
    rep = lax.axis_index("rep")
    y, x = rep // SIDE, rep % SIDE
    core = lax.axis_index("shard") % 2
    return jnp.where(core == 0, x, y), jnp.where(core == 0, y, x), core


def block_of(early, late, core):
    return jnp.where(core == 0, late * SIDE + early, early * SIDE + late)


def params(mebibytes):
    return pltpu.CompilerParams(vmem_limit_bytes=mebibytes * 1024 * 1024)


def block_columns(block):
    return pl.ds(pl.multiple_of(block * COLS, COLS), COLS)


def split_kernel(wanted, grads, *refs):
    outs, sems = refs[:-1], refs[-1]
    early, late, core = place()
    copies = []
    for out, steps in zip(outs, wanted):
        for number, (early_step, late_step) in enumerate(steps):
            block = block_of((early + early_step) % SIDE, (late + late_step) % SIDE, core)
            source = grads.at[:, :, block_columns(block)]
            copies.append(pltpu.make_async_copy(source, out.at[number], sems.at[len(copies)]))
    for copy in copies:
        copy.start()
    for copy in copies:
        copy.wait()


def split(grads, wanted, mebibytes):
    return pl.pallas_call(
        lambda *refs: split_kernel(wanted, *refs),
        out_shape=[jax.ShapeDtypeStruct((len(steps), MATS, ROWS, COLS), BF) for steps in wanted],
        in_specs=[pl.BlockSpec(memory_space=pl.ANY)],
        out_specs=[pl.BlockSpec(memory_space=pltpu.VMEM)] * len(wanted),
        scratch_shapes=[pltpu.SemaphoreType.DMA((sum(len(steps) for steps in wanted),))],
        compiler_params=params(mebibytes),
        name="split",
    )(grads)


def add(*parts):
    total = parts[0].astype(F32)
    for part in parts[1:]:
        total = total + part.astype(F32)
    return total


def panel_spans():
    return [(low, min(PANEL, FF - low)) for low in range(0, FF, PANEL)]


def panel_product(columns, low, size):
    return lax.dot_general(
        columns[low:, :], columns[low : low + size, :], (((1,), (1,)), ((), ())), preferred_element_type=F32
    )


def bring(pieces, columns, sems):
    copies = []
    for number, halves in enumerate(pieces):
        for half, piece in enumerate(halves):
            target = columns.at[pl.ds(half * HALF, HALF), pl.ds(number * COLS, COLS)]
            copies.append(pltpu.make_async_copy(piece, target, sems.at[number, half]))
    for copy in copies:
        copy.start()
    return copies


def flat(refs):
    views, upper = [], None
    for ref in refs:
        if ref.shape[1] == FF:
            views += [tuple(ref.at[n, pl.ds(half * HALF, HALF)] for half in range(2)) for n in range(ref.shape[0])]
        elif upper is None:
            upper = ref
        else:
            views += [(upper.at[n], ref.at[n]) for n in range(ref.shape[0])]
            upper = None
    return views


def gram_kernel(stacks, before, *refs):
    spans = panel_spans()
    pieces, refs = flat(refs[:stacks]), refs[stacks:]
    old, refs = (refs[: len(spans)], refs[len(spans) :]) if before else (None, refs)
    new, (columns, sems) = refs[: len(spans)], refs[len(spans) :]
    for copy in bring(pieces, columns, sems):
        copy.wait()
    for number, (low, size) in enumerate(spans):
        product = panel_product(columns, low, size)
        new[number][...] = product + old[number][...] if before else product


def gram_part(pieces, before=()):
    count = sum(piece.shape[0] * piece.shape[1] for piece in pieces) // FF
    inside = pl.BlockSpec(memory_space=pltpu.VMEM)
    return pl.pallas_call(
        lambda *refs: gram_kernel(len(pieces), bool(before), *refs),
        out_shape=[jax.ShapeDtypeStruct((FF - low, size), F32) for low, size in panel_spans()],
        in_specs=[pl.BlockSpec(memory_space=pl.ANY)] * len(pieces) + [inside] * len(before),
        out_specs=[inside] * len(panel_spans()),
        scratch_shapes=[pltpu.VMEM((FF, count * COLS), BF), pltpu.SemaphoreType.DMA((count, 2))],
        compiler_params=params(16),
        name="gram",
    )(*pieces, *before)


def newton_kernel(stacks, places, fresh_at, *refs):
    spans = panel_spans()
    pieces, refs = flat(refs[:stacks]), refs[stacks:]
    before, refs = refs[: len(spans)], refs[len(spans) :]
    own, rows_out, cols_out, whole, fresh, gram, sems, fresh_sems = refs
    early, late, core = place()
    floor = lax.axis_index("shard") // 2
    rep = block_of(early, late, core)
    fresh_copies = bring([pieces[number] for number in fresh_at], fresh, fresh_sems)
    copies = []
    for number, (k, j) in enumerate(places):
        block = block_of((early - k + SIDE) % SIDE, (late - j + SIDE) % SIDE, core)
        for part, piece in enumerate(pieces[number]):
            target = whole.at[pl.ds(part * HALF, HALF), block_columns(block)]
            copies.append(pltpu.make_async_copy(piece, target, sems.at[number, part]))
    for copy in copies:
        copy.start()
    start = own[...].astype(F32).T
    for copy in fresh_copies:
        copy.wait()
    squares = jnp.zeros((), F32)
    for number, (low, size) in enumerate(spans):
        panel = panel_product(fresh, low, size)
        panel = panel + before[number][...]
        on_line = lax.broadcasted_iota(jnp.int32, (size, size), 0) == lax.broadcasted_iota(
            jnp.int32, (size, size), 1
        )
        squares = squares + jnp.sum(jnp.where(on_line, panel[:size], 0.0))
        panel = panel.astype(BF)
        gram[low:, low : low + size] = panel
        if low + size < FF:
            gram[low : low + size, low + size :] = panel[size:].T
    factor = spectral_gain * math.sqrt(FF * D) / jnp.sqrt(jnp.full((1, 1), squares) + epsilon)
    scale = factor * factor / D
    half = rep % 2
    layer = (floor - rep // 4 + SIDE) % SIDE
    flipped = (rep // 2 % 2 + core) % 2
    base = layer * (2 * ROWS) + flipped * ROWS + half * (STRIP - 8)

    def strip_of(ref):
        window = ref[pl.ds(pl.multiple_of(base, 16), STRIP + 8), :].astype(F32)
        return jnp.where(half == 0, window[:STRIP], window[8:])

    first = scale * jnp.dot(start.astype(BF), gram[...], preferred_element_type=F32)
    strip = scale * strip_of(gram)
    power = jnp.concatenate([first, strip], axis=0)
    for _ in range(3):
        product = jnp.dot(power.astype(BF), gram[...], preferred_element_type=F32)
        power = 1.5 * power - (0.5 * scale) * product
    mixed = (0.75 * strip + 0.5 * power[COLS:]).astype(BF)
    for copy in copies:
        copy.wait()
    product = jnp.dot(mixed, whole[...], preferred_element_type=F32)
    rows_out[...] = (factor * (2.25 * strip_of(whole) - product)).astype(BF)
    columns = (factor * (2.25 * start - 0.75 * first - 0.5 * power[:COLS])).T.astype(BF)
    for k in range(SIDE):
        for i in range(2):
            at = ((floor - k + SIDE) % SIDE * 2 + (core + i) % 2) * ROWS
            low = (2 * k + i) * ROWS
            cols_out[pl.ds(pl.multiple_of(at, 16), ROWS), :] = columns[low : low + ROWS]


def newton(pieces, places, fresh_at, before, own):
    anywhere = pl.BlockSpec(memory_space=pl.ANY)
    inside = pl.BlockSpec(memory_space=pltpu.VMEM)
    return pl.pallas_call(
        lambda *refs: newton_kernel(len(pieces), places, fresh_at, *refs),
        out_shape=[jax.ShapeDtypeStruct((STRIP, D), BF), jax.ShapeDtypeStruct((FF, COLS), BF)],
        in_specs=[anywhere] * len(pieces) + [inside] * (len(before) + 1),
        out_specs=[inside, inside],
        scratch_shapes=[
            pltpu.VMEM((FF, D), BF),
            pltpu.VMEM((FF, len(fresh_at) * COLS), BF),
            pltpu.VMEM((FF, FF), BF),
            pltpu.SemaphoreType.DMA((16, 2)),
            pltpu.SemaphoreType.DMA((len(fresh_at), 2)),
        ],
        compiler_params=params(24),
        name="newton",
    )(*pieces, *before, own)


def slots_of(owner, who):
    mine = owner == who
    count = jnp.sum(mine.astype(jnp.int32))
    index = jnp.arange(MATS, dtype=jnp.int32)
    first = jnp.min(jnp.where(mine, index, MATS))
    last = jnp.max(jnp.where(mine, index, -1))
    return (jnp.where(count > 0, first, 0), count > 0), (jnp.where(count > 1, last, 0), count > 1)


def choose_kernel(count, choice, *refs):
    pieces, rest = refs[:count], refs[count:]
    out = rest[len(rest) // 2]
    if len(rest) == 3:
        rest[2][...] = rest[0][...]
    for slot in range(CAP):
        for number, piece in enumerate(pieces):

            @pl.when(choice[slot] == number)
            def _():
                out[0, slot] = piece[...] if len(piece.shape) == 2 else piece[0, slot]

        @pl.when(choice[slot] == count)
        def _():
            out[0, slot] = jnp.zeros((STRIP, D), BF)


def choose(choice, pieces, *along):
    inside = pl.BlockSpec(memory_space=pltpu.VMEM)
    return pl.pallas_call(
        lambda *refs: choose_kernel(len(pieces), *refs),
        out_shape=[
            jax.ShapeDtypeStruct((1, CAP, STRIP, D), BF),
            *[jax.ShapeDtypeStruct(array.shape, array.dtype) for array in along],
        ],
        in_specs=[pl.BlockSpec(memory_space=pltpu.SMEM)] + [inside] * (len(pieces) + len(along)),
        out_specs=[inside] * (1 + len(along)),
        compiler_params=params(6),
        name="choose",
    )(jnp.stack(choice).astype(jnp.int32), *pieces, *along)


def per_device(grads, momentum, owner):
    grads = grads[0]
    axes = ("rep", "shard")

    def move(piece, phase, step):
        return lax.ppermute(piece, axes, along(phase, step))

    def cut(*wanted, mebibytes=4):
        return split(grads, [[(early, late) for late in lates] for early, lates in wanted], mebibytes)

    one, two = (3, 0), (2, 1)
    (across_one,), (across_two,) = cut((2, one), mebibytes=58), cut((2, two), mebibytes=58)
    across_one, across_two = move(across_one, 0, 1), move(across_two, 0, 3)
    side_one, side_two = cut((3, one), (1, two))
    side_two, side_one = move(side_two, 0, 1), move(side_one, 0, 3)
    next_one, next_two = cut((1, one), (3, two))
    mine_one, mine_two = cut((0, one), (0, two))
    relay_one = move(add(next_one, across_one).astype(BF), 0, 1)
    relay_two = move(add(next_two, across_two).astype(BF), 0, 3)
    sums = [add(mine_two[n], relay_two[n], side_two[n]).astype(BF) for n in range(2)]
    sums.append(add(mine_one[0], relay_one[0], side_one[0]).astype(BF))
    sum_2, sum_1, sum_3 = lax.optimization_barrier(sums)
    late_2, late_1, late_3 = move(sum_2, 1, 2), move(sum_1, 1, 1), move(sum_3, 1, 3)
    terms = (mine_one[1], relay_one[1], side_one[1], late_2, late_1, late_3)
    summed = add(*terms)
    rounded = (summed + decay_rate * (decay_rate * momentum + summed)).astype(BF)
    shard = lax.axis_index("shard")
    floor, core = shard // 2, shard % 2
    swap = [(s, s ^ 1) for s in range(8)]
    by_core = rounded.reshape(SIDE, 2, ROWS, COLS)
    mine = lax.dynamic_index_in_dim(by_core, core, 1, keepdims=False)
    theirs = lax.dynamic_index_in_dim(by_core, 1 - core, 1, keepdims=False)
    layers = jnp.stack([mine, lax.ppermute(theirs, "shard", swap)], axis=1)

    def layer(step):
        return lax.dynamic_index_in_dim(layers, (floor + step) % SIDE, 0, keepdims=False)

    part_2, part_1, part_3 = [lax.ppermute(layer(n), "shard", along_z(n)) for n in (2, 1, 3)]
    own = jnp.stack([layer(0), part_1, part_2, part_3]).reshape(FF, COLS)
    line_1, line_3, line_2 = move(own, 0, 1), move(own, 0, 3), move(own, 0, 2)
    line = jnp.stack([own, line_1, line_3, line_2])
    halves = [line[:, :HALF], line[:, HALF:]]
    aheads, behinds = [move(half, 1, 1) for half in halves], [move(half, 1, 3) for half in halves]
    terms, _ = lax.optimization_barrier((terms, line))
    new_momentum = decay_rate * momentum + add(*terms)
    gram = gram_part([line])
    aheads[1], behinds[1], gram, new_momentum = lax.optimization_barrier((aheads[1], behinds[1], gram, new_momentum))
    across_as = [move(ahead[:2], 1, 1) for ahead in aheads]
    across_bs = [move(behind[2:], 1, 3) for behind in behinds]
    gram = gram_part([*aheads, *behinds], gram)
    pieces = [line, *aheads, *behinds, *across_as, *across_bs]
    places = [(k, j) for j in (0, 1, 3, 2) for k in (0, 1, 3, 2)]
    strip, columns = newton(pieces, places, (12, 13, 14, 15), gram, own)
    strip_2, strip_1, strip_3 = [lax.ppermute(strip, "shard", along_z(n)) for n in (2, 1, 3)]
    pieces = [strip, strip_1, strip_2, strip_3]
    update = lax.all_to_all(columns.reshape(MATS, ROWS, COLS), "shard", 0, 0, tiled=True)
    pieces, update = lax.optimization_barrier((pieces, update))
    wanted = [(floor - m // 2 + 4) % 4 for m, _ in slots_of(owner, floor * 2 + 1 - core)]
    handed = lax.ppermute(choose(wanted, pieces)[0], "shard", swap)
    choice = []
    for m, filled in slots_of(owner, shard):
        choice.append(jnp.where(filled, jnp.where(m % 2 == core, (floor - m // 2 + 4) % 4, 4), 5))
    owned, update = choose(choice, [*pieces, handed], update)
    return new_momentum, update, owned


def solution(mesh):
    placed = (P("rep", None, "shard", None), P(None, "shard", "rep"), P())
    return jax.shard_map(
        per_device,
        mesh=mesh,
        in_specs=placed,
        out_specs=(P(None, "shard", "rep"), P(None, "shard", "rep"), P("shard", None, "rep", None)),
        check_vma=False,
    )
```
